32 devices in a mesh: row: 4 (over z), col: 8 (over y, x, core).
Axes of the slice: x: 2, y: 2, z: 4, core: 2. Of those that a mesh axis runs over, the one named last changes fastest.
Arguments:
- images: bfloat16 [8, 32, 65536], P(None, 'row', 'col'), may hold values from -6 to 6
- kernel: bfloat16 [3, 3, 1024, 1024], P(None, None, 'col', 'row'), may hold values from -0.09375 to 0.09375
- upstream: bfloat16 [8, 32, 65536], P(None, 'row', 'col'), may hold values from -6 to 6
Outputs:
- output_maps: bfloat16 [8, 32, 65536], P(None, 'row', 'col')
- input_grad: bfloat16 [8, 32, 65536], P(None, 'row', 'col')
- kernel_grad: float32 [3, 3, 1024, 1024], P(None, None, 'col', 'row')
The draws below stay inside these ranges and needn't reach their ends.
All inputs are finite; a program needn't handle non-finite values.
Results may differ from the reference program's by a relative error of at most 0.001.
Values may be sent and summed in bfloat16 or wider, within the bound.
A program may use at most 128 MiB of HBM per device.

```python
import jax
import jax.numpy as jnp
from jax import lax

CIN = 1024
COUT = 1024
W = 64
IMAGES = 8
H = 32


def with_spikes(array, own_key, source, target, shards_of, factor):
    owner, partner = [(jnp.arange(array.shape[dim]) // (array.shape[dim] // shards_of)).reshape([-1 if axis == dim else 1 for axis in range(array.ndim)]) for dim in (source, target)]
    chosen = jax.random.permutation(own_key, shards_of)[partner]
    strong = (owner == chosen) | (owner == (partner + shards_of // 2) % shards_of)
    return jnp.where(strong, factor * array, array)


def shard_levels(stream_key, extent, cuts, smallest, largest):
    loudness, own = 1.0, jax.random.fold_in(stream_key, 6)
    for position, parts in cuts:
        steps = jnp.exp(jax.random.uniform(jax.random.fold_in(own, position), (parts,), jnp.float32, smallest / len(cuts), largest / len(cuts)))
        loudness = loudness * jnp.repeat(steps, extent[position] // parts).reshape([-1 if axis == position else 1 for axis in range(len(extent))])
    return loudness


def normal_values(stream_key, shape, scale, bound, split=(), kind=jnp.bfloat16):
    level = shard_levels(stream_key, shape, split, -0.22, 0.18) if split else 1.0
    drawn = jax.random.normal(stream_key, shape, jnp.float32) * scale * level
    return jnp.minimum(jnp.maximum(drawn, -bound), bound).astype(kind)


def bell_draw_with(key, shape, spread, most, pieces, heavy, dtype=jnp.bfloat16):
    result = spread * jax.random.normal(key, shape, jnp.float32)
    if pieces:
        result = result * shard_levels(key, shape, pieces, -0.22, 0.18)
    return jnp.clip(with_spikes(result, jax.random.fold_in(key, 3), *heavy), -most, most).astype(dtype)


def setup_inputs(seed: int = 0) -> dict:
    seeds = jax.random.split(jax.random.key(seed), 4)
    return {
        "images": bell_draw_with(seeds[0], (IMAGES, H, CIN * W), 1.0, 6.0, ((1, 4), (2, 8)), (1, 2, 8, 2.0)),
        "kernel": bell_draw_with(seeds[1], (3, 3, COUT, CIN), (9 * CIN) ** -0.5, 0.09375, ((2, 8), (3, 4)), (2, 3, 8, 2.0)),
        "upstream": normal_values(seeds[2], (IMAGES, H, COUT * W), 1.0, 6.0, ((1, 4), (2, 8))),
    }


def convolve(inputs, weights):
    return lax.conv_general_dilated(inputs.astype(jnp.float32), weights.astype(jnp.float32), (1, 1), ((1, 1), (1, 1)), dimension_numbers=("NHWC", "HWIO", "NHWC"), precision=lax.Precision.HIGHEST)


def to_maps(flat, channels):
    return flat.reshape(flat.shape[0], flat.shape[1], channels, W).transpose(0, 1, 3, 2)


def to_flat(maps):
    return maps.transpose(0, 1, 3, 2).reshape(maps.shape[0], maps.shape[1], maps.shape[3] * maps.shape[2])


def reference(images, kernel, upstream):
    inputs = to_maps(images, CIN)
    gradient_maps = to_maps(upstream, COUT)
    hwio = kernel.transpose(0, 1, 3, 2)
    output_maps = to_flat(convolve(inputs, hwio)).astype(jnp.bfloat16)
    turned = jnp.flip(kernel, (0, 1))
    input_grad = to_flat(convolve(gradient_maps, turned)).astype(jnp.bfloat16)
    padded = jnp.pad(inputs.astype(jnp.float32), ((0, 0), (1, 1), (1, 1), (0, 0)))
    gradient = gradient_maps.astype(jnp.float32)
    height = inputs.shape[1]
    width = inputs.shape[2]
    rows_list = []
    for tap_row in range(3):
        cols_list = []
        for tap_col in range(3):
            window = padded[:, tap_row:tap_row + height, tap_col:tap_col + width, :]
            cols_list.append(jnp.einsum("bhwi,bhwo->oi", window, gradient, precision=lax.Precision.HIGHEST))
        rows_list.append(jnp.stack(cols_list))
    kernel_grad = jnp.stack(rows_list)
    return output_maps, input_grad, kernel_grad
```

```python
import functools

import jax
import jax.numpy as jnp
from jax import lax
from jax.experimental import pallas as pl
from jax.experimental.pallas import tpu as pltpu
from jax.sharding import PartitionSpec as P

W = 64
MESH = pl.DeviceIdType.MESH
F32 = jnp.float32
BF16 = jnp.bfloat16


def remote(src, dst, send, recv, row, col):
    return pltpu.make_async_remote_copy(
        src_ref=src, dst_ref=dst, send_sem=send, recv_sem=recv, device_id=(row, col), device_id_type=MESH
    )


def shift_sum(low, mid, high, width):
    rows = low.shape[0]
    at = lax.rem(lax.broadcasted_iota(jnp.int32, low.shape, 0), jnp.int32(width))
    first = jnp.where(at == 0, 0.0, pltpu.roll(low, 1, 0))
    last = jnp.where(at == width - 1, 0.0, pltpu.roll(high, rows - 1, 0))
    return first + mid + last


def kernel(
    n_row, x_ref, g_ref, w_ref, out_ref, ig_ref, kg_ref,
    xg, gg, wf, wb, halo, turned, kgp, kgr, kgz, stage,
    own_sem, ax_send, ax_recv, hz_send, hz_recv, hc_send, hc_recv,
    wz_send, wz_recv, wp_send, wp_recv, wc_send, wc_recv, wq_send, wq_recv,
    kp_send, kp_recv, kz_send, kz_recv, op_send, op_recv,
):
    batch, height, width, ch = x_ref.shape
    half = batch // 2
    pair = 2 * ch
    taps = w_ref.shape[0]
    row, col = lax.axis_index("row"), lax.axis_index("col")
    chip, core = col // 2, lax.rem(col, 2)
    mate = chip * 2 + 1 - core

    def chip_at(t):
        cx, cy = lax.rem(chip, 2), chip // 2
        return lax.rem(cy + t // 2, 2) * 2 + lax.rem(cx + t % 2, 2)

    chips = [chip_at(t) for t in range(4)]
    peers = [(t, k) for t in range(4) for k in range(2) if (t, k) != (0, 0)]

    def peer(t, k):
        return chips[t] * 2 + lax.rem(core + k, 2)

    def row_at(s):
        return lax.rem(row + s, n_row)

    barrier = pltpu.get_barrier_semaphore()
    for t, k in peers:
        pl.semaphore_signal(barrier, inc=1, device_id=(row, peer(t, k)), device_id_type=MESH)
    for s in range(1, n_row):
        pl.semaphore_signal(barrier, inc=1, device_id=(row_at(s), col), device_id_type=MESH)
    pl.semaphore_wait(barrier, len(peers) + n_row - 1)

    def lanes(c, size):
        return pl.ds(pl.multiple_of(c * size, size), size)

    own = pl.ds(core * half, half)
    arrays = ((x_ref, xg), (g_ref, gg))
    has_up, has_down = row > 0, row < n_row - 1

    def body_copy(n, t, k, source):
        src, dst = arrays[n]
        to = peer(t, k)
        return remote(
            src.at[pl.ds(lax.rem(core + k, 2) * half, half)],
            dst.at[:, pl.ds(1, height), :, lanes(source, ch)],
            ax_send.at[n, t, k], ax_recv.at[n, t, k], row, to,
        )

    def halo_z(n, side):
        src, _ = arrays[n]
        at = height - 1 if side == 0 else 0
        to = row + 1 if side == 0 else row - 1
        return remote(src.at[:, pl.ds(at, 1)], halo.at[n, side], hz_send.at[n, side], hz_recv.at[n, side], to, col)

    def halo_c(n, side, t, k, source):
        _, dst = arrays[n]
        at = 0 if side == 0 else height + 1
        return remote(
            halo.at[n, side, pl.ds(lax.rem(core + k, 2) * half, half)],
            dst.at[:, pl.ds(at, 1), :, lanes(source, ch)],
            hc_send.at[n, side, t, k], hc_recv.at[n, side, t, k], row, peer(t, k),
        )

    def halo_own(n, side):
        _, dst = arrays[n]
        at = 0 if side == 0 else height + 1
        return pltpu.make_async_copy(
            halo.at[n, side, own], dst.at[:, pl.ds(at, 1), :, lanes(col, ch)], hc_send.at[n, side, 0, 0]
        )

    def weights_z(s, source):
        return remote(
            w_ref, wf.at[:, lanes(core, ch), lanes(source, pair)], wz_send.at[s], wz_recv.at[s], row_at(s), col
        )

    def has(side):
        return has_up if side == 0 else has_down

    @pl.when(has_down)
    def _():
        for n in range(2):
            halo_z(n, 0).start()

    @pl.when(has_up)
    def _():
        for n in range(2):
            halo_z(n, 1).start()

    own_copies = [
        pltpu.make_async_copy(x_ref.at[own], xg.at[:, pl.ds(1, height), :, lanes(col, ch)], own_sem.at[0]),
        pltpu.make_async_copy(g_ref.at[own], gg.at[:, pl.ds(1, height), :, lanes(col, ch)], own_sem.at[1]),
        pltpu.make_async_copy(w_ref, wf.at[:, lanes(core, ch), lanes(row, pair)], own_sem.at[2]),
    ]
    for copy in own_copies:
        copy.start()
    body_copy(1, 0, 1, col).start()
    for t, k in peers:
        body_copy(0, t, k, col).start()
    for s in range(1, n_row):
        weights_z(s, row).start()

    @pl.when(jnp.logical_not(has_up))
    def _():
        xg[:, 0] = jnp.zeros((half, width, xg.shape[3]), BF16)
        gg[:, 0] = jnp.zeros((half, width, xg.shape[3]), BF16)

    @pl.when(jnp.logical_not(has_down))
    def _():
        xg[:, height + 1] = jnp.zeros((half, width, xg.shape[3]), BF16)
        gg[:, height + 1] = jnp.zeros((half, width, xg.shape[3]), BF16)

    def spread_halo(n):
        for side in range(2):
            @pl.when(has(side))
            def _():
                halo_z(n, side).wait_recv()
                halo_own(n, side).start()
                for t, k in peers:
                    halo_c(n, side, t, k, col).start()

    spread_halo(0)
    for t, k in peers:
        if t:
            body_copy(1, t, k, col).start()
    spread_halo(1)

    own_copies[0].wait()
    own_copies[1].wait()
    body_copy(1, 0, 1, mate).wait_recv()

    def turn(b, _):
        block = gg[b, pl.ds(1, height), :, lanes(chip, pair)].astype(F32).reshape(height * width, pair)
        at = lax.rem(lax.broadcasted_iota(jnp.int32, block.shape, 0), jnp.int32(width))
        rows = height * width
        left = jnp.where(at == width - 1, 0.0, pltpu.roll(block, rows - 1, 0))
        right = jnp.where(at == 0, 0.0, pltpu.roll(block, 1, 0))
        where = pl.ds(pl.multiple_of(b * rows, rows), rows)
        for c, part in enumerate((left, block, right)):
            turned[c * pair:(c + 1) * pair, where] = part.T.astype(BF16)
        return 0

    lax.fori_loop(0, half, turn, 0)

    def wait_halos(n, t):
        for side in range(2):
            @pl.when(has(side))
            def _():
                for k in range(2):
                    if (t, k) == (0, 0):
                        halo_own(n, side).wait()
                    else:
                        halo_c(n, side, t, k, peer(t, k)).wait_recv()

    def mate_part(t):
        theirs = pl.ds(pl.multiple_of((1 - core) * ch, ch), ch)
        return remote(kgp.at[t, :, theirs], kgr.at[t], kp_send.at[t], kp_recv.at[t], row, mate)

    def z_part(t, to, slot):
        mine = pl.ds(pl.multiple_of(core * ch, ch), ch)
        return remote(kgp.at[t, :, mine], kgz.at[slot], kz_send.at[t], kz_recv.at[slot], to, col)

    def hand_on(t):
        mate_part(t).wait_recv()
        mine = pl.ds(pl.multiple_of(core * ch, ch), ch)

        def add(i, _):
            kgp[t, i, mine] = kgp[t, i, mine] + kgr[t, i]
            return 0

        lax.fori_loop(0, taps, add, 0)

        @pl.when(chips[t] != row)
        def _():
            z_part(t, chips[t], row).start()

        @pl.when(chips[t] == row)
        def _():
            def keep(i, _):
                kg_ref[i] = kgp[t, i, mine]
                return 0

            lax.fori_loop(0, taps, keep, 0)

    for t in range(4):
        for k in range(2):
            if (t, k) != (0, 0):
                body_copy(0, t, k, peer(t, k)).wait_recv()
        wait_halos(0, t)

        def tap_row(a, _):
            window = xg[:, pl.ds(a, height), :, lanes(chips[t], pair)].reshape(half * height * width, pair)
            part = jnp.dot(turned[...], window, preferred_element_type=F32)
            for c in range(3):
                kgp[t, a * 3 + c] = part[c * pair:(c + 1) * pair]
            return 0

        lax.fori_loop(0, 3, tap_row, 0)
        mate_part(t).start()
        if t:
            hand_on(t - 1)
    hand_on(3)

    own_copies[2].wait()
    for s in range(1, n_row):
        weights_z(s, lax.rem(row + n_row - s, n_row)).wait_recv()

    def weights_mate(k):
        mine = lanes(core if k == 0 else 1 - core, ch)
        return remote(wf.at[:, mine], wf.at[:, mine], wp_send, wp_recv, row, mate)

    def weights_c(t, source):
        return remote(
            wf.at[:, lanes(core, ch), lanes(chips[t], pair)], wb.at[:, lanes(source, ch)],
            wc_send.at[t], wc_recv.at[t], row, peer(t, 0),
        )

    weights_mate(0).start()
    wb_own = pltpu.make_async_copy(wf.at[:, lanes(core, ch), lanes(chip, pair)], wb.at[:, lanes(col, ch)], own_sem.at[3])
    wb_own.start()
    for t in range(1, 4):
        weights_c(t, col).start()

    def weights_pass(t, k):
        rows = lanes(peer(t, k), ch)
        return remote(wb.at[:, rows], wb.at[:, rows], wq_send.at[t], wq_recv.at[t], row, mate)

    def convolve(grid_ref, weights, dims, flip, result, n):
        def image(b, _):
            sums = []
            for c in range(3):
                total = None
                for a in range(3):
                    block = grid_ref[b, pl.ds(2 - a if flip else a, height)].reshape(height * width, grid_ref.shape[3])
                    part = lax.dot_general(block, weights[a * 3 + c], (dims, ((), ())), preferred_element_type=F32)
                    total = part if total is None else total + part
                sums.append(total)
            if flip:
                sums = sums[::-1]
            value = shift_sum(*sums, width).astype(BF16).reshape(height, width, pair)

            @pl.when(core == 0)
            def _():
                result[b] = value[:, :, :ch]
                stage[n, b] = value[:, :, ch:]

            @pl.when(core == 1)
            def _():
                result[half + b] = value[:, :, ch:]
                stage[n, b] = value[:, :, :ch]

            return 0

        lax.fori_loop(0, half, image, 0)

    def result_mate(n, result, batch_half):
        return remote(
            stage.at[n], result.at[pl.ds(batch_half * half, half)], op_send.at[n], op_recv.at[n], row, mate
        )

    weights_mate(1).wait_recv()
    convolve(xg, wf, ((1,), (1,)), False, out_ref, 0)
    result_mate(0, out_ref, core).start()

    wb_own.wait()
    weights_pass(0, 0).start()
    for t in range(1, 4):
        weights_c(t, peer(t, 0)).wait_recv()
        weights_pass(t, 0).start()
    for t in range(1, 4):
        for k in range(2):
            body_copy(1, t, k, peer(t, k)).wait_recv()
    for t in range(4):
        wait_halos(1, t)
    for t in range(4):
        weights_pass(t, 1).wait_recv()
    convolve(gg, wb, ((1,), (0,)), True, ig_ref, 1)
    result_mate(1, ig_ref, core).start()

    for s in range(1, n_row):
        z_part(0, row, row_at(s)).wait_recv()

        def add(i, _):
            kg_ref[i] = kg_ref[i] + kgz[row_at(s), i]
            return 0

        lax.fori_loop(0, taps, add, 0)

    for n in range(2):
        for t, k in peers:
            body_copy(n, t, k, col).wait_send()
        for side in range(2):
            @pl.when(has(1 - side))
            def _():
                halo_z(n, side).wait_send()

            @pl.when(has(side))
            def _():
                for t, k in peers:
                    halo_c(n, side, t, k, col).wait_send()
    for s in range(1, n_row):
        weights_z(s, row).wait_send()
    weights_mate(0).wait_send()
    for t in range(1, 4):
        weights_c(t, col).wait_send()
    for t in range(4):
        weights_pass(t, 0).wait_send()
        mate_part(t).wait_send()

        @pl.when(chips[t] != row)
        def _():
            z_part(t, chips[t], row).wait_send()

    result_mate(0, out_ref, core).wait_send()
    result_mate(1, ig_ref, core).wait_send()
    result_mate(0, out_ref, 1 - core).wait_recv()
    result_mate(1, ig_ref, 1 - core).wait_recv()


def fused(images, upstream, weights):
    n_row, n_col = lax.axis_size("row"), lax.axis_size("col")
    batch, height, width, ch = images.shape
    taps, pair, half = weights.shape[0], 2 * ch, batch // 2
    every = ch * n_col
    dma = pltpu.SemaphoreType.DMA
    vmem = pl.BlockSpec(memory_space=pltpu.VMEM)
    grid = (half, height + 2, width, every)
    flops = 3 * 2 * half * height * width * every * pair * taps
    return pl.pallas_call(
        functools.partial(kernel, n_row),
        out_shape=(
            jax.ShapeDtypeStruct(images.shape, BF16),
            jax.ShapeDtypeStruct(images.shape, BF16),
            jax.ShapeDtypeStruct(weights.shape, F32),
        ),
        in_specs=[vmem] * 3,
        out_specs=(vmem,) * 3,
        scratch_shapes=[
            pltpu.VMEM(grid, BF16),
            pltpu.VMEM(grid, BF16),
            pltpu.VMEM((taps, pair, every), BF16),
            pltpu.VMEM((taps, every, pair), BF16),
            pltpu.VMEM((2, 2, batch, 1, width, ch), BF16),
            pltpu.VMEM((3 * pair, half * height * width), BF16),
            pltpu.VMEM((4, taps, pair, pair), F32),
            pltpu.VMEM((4, taps, ch, pair), F32),
            pltpu.VMEM((n_row, taps, ch, pair), F32),
            pltpu.VMEM((2, half, height, width, ch), BF16),
            dma((4,)),
            dma((2, 4, 2)), dma((2, 4, 2)),
            dma((2, 2)), dma((2, 2)),
            dma((2, 2, 4, 2)), dma((2, 2, 4, 2)),
            dma((n_row,)), dma((n_row,)),
            dma, dma,
            dma((4,)), dma((4,)),
            dma((4,)), dma((4,)),
            dma((4,)), dma((4,)),
            dma((4,)), dma((n_row,)),
            dma((2,)), dma((2,)),
        ],
        compiler_params=pltpu.CompilerParams(
            collective_id=0, has_side_effects=True, vmem_limit_bytes=60 * 1024 * 1024
        ),
        cost_estimate=pl.CostEstimate(flops=flops, bytes_accessed=8 * 1024 * 1024, transcendentals=0),
    )(images, upstream, weights)


def fits(n_row, n_col, images, kernel_block):
    ch = images.shape[2] // W
    return (
        n_row == 4 and n_col == 8 and ch == 128 and images.shape[0] % 2 == 0
        and kernel_block.shape[2] == ch and kernel_block.shape[3] == 2 * ch and images.size <= 8 * 8 * 8192
    )


def to_last(flat):
    return to_maps(flat).transpose(0, 1, 3, 2)


def from_last(maps):
    return to_flat(maps.transpose(0, 1, 3, 2))


def padded_2(block, sides, width):
    for axis, dim in sides:
        count = lax.axis_size(axis)
        forward = [(i, i + 1) for i in range(count - 1)]
        backward = [(target, source) for source, target in forward]
        low = lax.ppermute(
            lax.slice_in_dim(block, block.shape[dim] - width, None, axis=dim), axis, forward
        )
        high = lax.ppermute(lax.slice_in_dim(block, 0, width, axis=dim), axis, backward)
        block = jnp.concatenate([low, block, high], axis=dim)
    return block


def convolve_valid(inputs, weights, weight_spec):
    return lax.conv_general_dilated(
        inputs,
        weights,
        (1, 1),
        ((0, 0), (1, 1)),
        dimension_numbers=("NHCW", weight_spec, "NHCW"),
        preferred_element_type=jnp.float32,
    )


def to_maps(flat):
    return flat.reshape(flat.shape[0], flat.shape[1], flat.shape[2] // W, W)


def to_flat(maps):
    return maps.reshape(maps.shape[0], maps.shape[1], maps.shape[2] * maps.shape[3])


def gathered(images, kernel, upstream):
    weights_all = lax.all_gather(kernel, "row", axis=3, tiled=True)
    images_rim = padded_2(images, (("row", 1),), 1)
    grads_rim = padded_2(upstream, (("row", 1),), 1)
    grads_maps = to_maps(grads_rim)
    batch = images.shape[0]
    height = images.shape[1]
    width = W
    out_local = kernel.shape[2]
    grads_mid = grads_maps[:, 1:-1]
    output_init = jnp.zeros((batch, height, out_local, width), jnp.float32)
    output_sum = output_init
    panel_in = to_maps(lax.all_gather(images_rim, "col", axis=2, tiled=True))
    count_here = panel_in.shape[2]
    output_sum = output_sum + convolve_valid(panel_in, weights_all, "HWOI")
    padded = jnp.pad(panel_in, ((0, 0), (0, 0), (0, 0), (1, 1)))
    blocks = []
    for tap_row in range(3):
        for tap_col in range(3):
            window = padded[:, tap_row : tap_row + height, :, tap_col : tap_col + width]
            blocks.append(
                jnp.einsum("bhiw,bhow->oi", window, grads_mid, preferred_element_type=jnp.float32)
            )
    stacked = jnp.stack(blocks).reshape(3, 3, out_local, count_here)
    output_sum, weight_part = (output_sum, stacked)
    kernel_grad = lax.psum_scatter(weight_part, "row", scatter_dimension=3, tiled=True)
    flipped = jnp.flip(weights_all, (0, 1))
    partial_grad = to_flat(convolve_valid(grads_maps, flipped, "HWIO"))
    input_grad = lax.psum_scatter(partial_grad, "col", scatter_dimension=2, tiled=True)
    return (to_flat(output_sum).astype(jnp.bfloat16), input_grad.astype(jnp.bfloat16), kernel_grad)


def shards(images, kernel_block, upstream):
    if not fits(lax.axis_size("row"), lax.axis_size("col"), images, kernel_block):
        return gathered(images, kernel_block, upstream)
    taps = kernel_block.reshape((9,) + kernel_block.shape[2:])
    out, grad, kernel_grad = fused(to_last(images), to_last(upstream), taps)
    return from_last(out), from_last(grad), kernel_grad.reshape(kernel_block.shape)


def solution(mesh):
    return jax.shard_map(
        shards,
        mesh=mesh,
        in_specs=(P(None, "row", "col"), P(None, None, "col", "row"), P(None, "row", "col")),
        out_specs=(P(None, "row", "col"), P(None, "row", "col"), P(None, None, "col", "row")),
        check_vma=False,
    )
```

```python
import functools

import jax
import jax.numpy as jnp
from jax import lax
from jax.experimental import pallas as pl
from jax.experimental.pallas import tpu as pltpu
from jax.sharding import PartitionSpec as P

W = 64
MESH = pl.DeviceIdType.MESH
F32 = jnp.float32
BF16 = jnp.bfloat16


def remote(src, dst, send, recv, row, col):
    return pltpu.make_async_remote_copy(
        src_ref=src, dst_ref=dst, send_sem=send, recv_sem=recv, device_id=(row, col), device_id_type=MESH
    )


def shift_sum(low, mid, high, width):
    rows = low.shape[0]
    at = lax.rem(lax.broadcasted_iota(jnp.int32, low.shape, 0), jnp.int32(width))
    first = jnp.where(at == 0, 0.0, pltpu.roll(low, 1, 0))
    last = jnp.where(at == width - 1, 0.0, pltpu.roll(high, rows - 1, 0))
    return first + mid + last


def kernel(
    n_row, x_ref, g_ref, w_ref, out_ref, ig_ref, kg_ref,
    xg, gg, wf, wb, halo, turned, kgp, kgr, kgz, stage,
    own_sem, ax_send, ax_recv, fx_send, fx_recv, hz_send, hz_recv, hc_send, hc_recv,
    wz_send, wz_recv, wp_send, wp_recv, wc_send, wc_recv, wq_send, wq_recv,
    kp_send, kp_recv, kz_send, kz_recv, op_send, op_recv,
):
    batch, height, width, ch = x_ref.shape
    half = batch // 2
    pair = 2 * ch
    taps = w_ref.shape[0]
    row, col = lax.axis_index("row"), lax.axis_index("col")
    chip, core = col // 2, lax.rem(col, 2)
    mate = chip * 2 + 1 - core

    def chip_at(t):
        cx, cy = lax.rem(chip, 2), chip // 2
        return lax.rem(cy + t // 2, 2) * 2 + lax.rem(cx + t % 2, 2)

    chips = [chip_at(t) for t in range(4)]
    every_peer = [(t, k) for t in range(4) for k in range(2) if (t, k) != (0, 0)]
    peers = [(t, k) for t, k in every_peer if t < 3]

    def peer(t, k):
        return chips[t] * 2 + lax.rem(core + k, 2)

    def row_at(s):
        return lax.rem(row + s, n_row)

    barrier = pltpu.get_barrier_semaphore()
    for t, k in every_peer:
        pl.semaphore_signal(barrier, inc=1, device_id=(row, peer(t, k)), device_id_type=MESH)
    for s in range(1, n_row):
        pl.semaphore_signal(barrier, inc=1, device_id=(row_at(s), col), device_id_type=MESH)
    pl.semaphore_wait(barrier, len(every_peer) + n_row - 1)

    def lanes(c, size):
        return pl.ds(pl.multiple_of(c * size, size), size)

    own = pl.ds(core * half, half)
    arrays = ((x_ref, xg), (g_ref, gg))
    has_up, has_down = row > 0, row < n_row - 1

    def body_copy(n, t, k, source):
        src, dst = arrays[n]
        to = peer(t, k)
        return remote(
            src.at[pl.ds(lax.rem(core + k, 2) * half, half)],
            dst.at[:, pl.ds(1, height), :, lanes(source, ch)],
            ax_send.at[n, t, k], ax_recv.at[n, t, k], row, to,
        )

    def halo_z(n, side):
        src, _ = arrays[n]
        at = height - 1 if side == 0 else 0
        to = row + 1 if side == 0 else row - 1
        return remote(src.at[:, pl.ds(at, 1)], halo.at[n, side], hz_send.at[n, side], hz_recv.at[n, side], to, col)

    def halo_c(n, side, t, k, source):
        _, dst = arrays[n]
        at = 0 if side == 0 else height + 1
        return remote(
            halo.at[n, side, pl.ds(lax.rem(core + k, 2) * half, half)],
            dst.at[:, pl.ds(at, 1), :, lanes(source, ch)],
            hc_send.at[n, side, t, k], hc_recv.at[n, side, t, k], row, peer(t, k),
        )

    def halo_own(n, side):
        _, dst = arrays[n]
        at = 0 if side == 0 else height + 1
        return pltpu.make_async_copy(
            halo.at[n, side, own], dst.at[:, pl.ds(at, 1), :, lanes(col, ch)], hc_send.at[n, side, 0, 0]
        )

    half_z = row // 2
    inner = (row == 1) | (row == 2)
    beside = row + 1 - 2 * lax.rem(row, 2)
    across = 2 - half_z
    far = 3 * (1 - half_z)
    blocks = [far, across, beside, row]

    def weights_z(source, index, to):
        part = wf.at[:, lanes(core, ch), lanes(source, pair)]
        return remote(part, part, wz_send.at[index], wz_recv.at[source], to, col)

    def weights_own(index, to):
        part = wf.at[:, lanes(core, ch), lanes(row, pair)]
        return remote(w_ref, part, wz_send.at[index], wz_recv.at[row], to, col)

    def pass_on(n, side):
        _, dst = arrays[n]
        part = dst.at[pl.ds(side * (half // 2), half // 2), :, :, lanes(chips[1 + side], pair)]
        return remote(part, part, fx_send.at[n, side], fx_recv.at[n, side], row, peer(2 - side, 0))

    def passed(n, side):
        _, dst = arrays[n]
        part = dst.at[pl.ds(side * (half // 2), half // 2), :, :, lanes(chips[3], pair)]
        return remote(part, part, fx_send.at[n, side], fx_recv.at[n, side], row, peer(2 - side, 0))

    def has(side):
        return has_up if side == 0 else has_down

    @pl.when(has_down)
    def _():
        for n in range(2):
            halo_z(n, 0).start()

    @pl.when(has_up)
    def _():
        for n in range(2):
            halo_z(n, 1).start()

    own_copies = [
        pltpu.make_async_copy(x_ref.at[own], xg.at[:, pl.ds(1, height), :, lanes(col, ch)], own_sem.at[0]),
        pltpu.make_async_copy(g_ref.at[own], gg.at[:, pl.ds(1, height), :, lanes(col, ch)], own_sem.at[1]),
        pltpu.make_async_copy(w_ref, wf.at[:, lanes(core, ch), lanes(row, pair)], own_sem.at[2]),
    ]
    for copy in own_copies:
        copy.start()
    body_copy(1, 0, 1, col).start()
    for t, k in peers:
        body_copy(0, t, k, col).start()
    weights_own(0, beside).start()

    @pl.when(inner)
    def _():
        weights_own(1, across).start()

    def clear(at):
        for t in range(3):
            for grid_ref in (xg, gg):
                grid_ref[:, at, :, lanes(chips[t], pair)] = jnp.zeros((half, width, pair), BF16)

    @pl.when(jnp.logical_not(has_up))
    def _():
        clear(0)

    @pl.when(jnp.logical_not(has_down))
    def _():
        clear(height + 1)

    def spread_halo(n):
        for side in range(2):
            @pl.when(has(side))
            def _():
                halo_z(n, side).wait_recv()
                halo_own(n, side).start()
                for t, k in peers:
                    halo_c(n, side, t, k, col).start()

    spread_halo(0)

    own_copies[0].wait()
    own_copies[1].wait()
    body_copy(1, 0, 1, mate).wait_recv()

    def turn(b, _):
        block = gg[b, pl.ds(1, height), :, lanes(chip, pair)].astype(F32).reshape(height * width, pair)
        at = lax.rem(lax.broadcasted_iota(jnp.int32, block.shape, 0), jnp.int32(width))
        rows = height * width
        left = jnp.where(at == width - 1, 0.0, pltpu.roll(block, rows - 1, 0))
        right = jnp.where(at == 0, 0.0, pltpu.roll(block, 1, 0))
        where = pl.ds(pl.multiple_of(b * rows, rows), rows)
        for c, part in enumerate((left, block, right)):
            turned[c * pair:(c + 1) * pair, where] = part.T.astype(BF16)
        return 0

    lax.fori_loop(0, half, turn, 0)

    def wait_halos(n, t):
        for side in range(2):
            @pl.when(has(side))
            def _():
                for k in range(2):
                    if (t, k) == (0, 0):
                        halo_own(n, side).wait()
                    else:
                        halo_c(n, side, t, k, peer(t, k)).wait_recv()

    def mate_part(t):
        theirs = pl.ds(pl.multiple_of((1 - core) * ch, ch), ch)
        return remote(kgp.at[t, :, theirs], kgr.at[t], kp_send.at[t], kp_recv.at[t], row, mate)

    mine = pl.ds(pl.multiple_of(core * ch, ch), ch)

    def z_part(t, to, slot):
        return remote(kgp.at[t, :, mine], kgz.at[slot], kz_send.at[t], kz_recv.at[slot], to, col)

    def add_in(t, other):
        def add(i, _):
            kgp[t, i, mine] = kgp[t, i, mine] + other[i]
            return 0

        lax.fori_loop(0, taps, add, 0)

    def pair_sum(t):
        mate_part(t).wait_recv()
        add_in(t, kgr.at[t])

    def relay(t):
        z_part(t, beside, t).wait_recv()
        add_in(t, kgz.at[t])
        z_part(t, blocks[t], 3).start()

    own_copies[2].wait()

    @pl.when(inner)
    def _():
        weights_z(beside, 2, across).wait_recv()
        weights_z(beside, 2, across).start()
        weights_z(across, 3, beside).wait_recv()
        weights_z(across, 3, beside).start()

    def neighbours(n):
        for t in range(3):
            for k in range(2):
                if t:
                    body_copy(n, t, k, peer(t, k)).wait_recv()
            wait_halos(n, t)
            if t:
                pass_on(n, t - 1).start()

    neighbours(0)
    for t, k in peers:
        if t:
            body_copy(1, t, k, col).start()
    spread_halo(1)

    @pl.when(inner)
    def _():
        weights_z(far, 4, beside).wait_recv()
        weights_z(far, 4, beside).start()

    @pl.when(jnp.logical_not(inner))
    def _():
        for source in (beside, across, far):
            weights_z(source, 0, beside).wait_recv()

    def weights_mate(k):
        mine = lanes(core if k == 0 else 1 - core, ch)
        return remote(wf.at[:, mine], wf.at[:, mine], wp_send, wp_recv, row, mate)

    def weights_c(t, source):
        return remote(
            wf.at[:, lanes(core, ch), lanes(chips[t], pair)], wb.at[:, lanes(source, ch)],
            wc_send.at[t], wc_recv.at[t], row, peer(t, 0),
        )

    weights_mate(0).start()
    wb_own = pltpu.make_async_copy(wf.at[:, lanes(core, ch), lanes(chip, pair)], wb.at[:, lanes(col, ch)], own_sem.at[3])
    wb_own.start()
    for t in range(1, 4):
        weights_c(t, col).start()
    body_copy(0, 0, 1, mate).wait_recv()
    passed(0, 0).wait_recv()
    passed(0, 1).wait_recv()

    for t in range(4):
        def tap_row(a, _):
            window = xg[:, pl.ds(a, height), :, lanes(blocks[t], pair)].reshape(half * height * width, pair)
            part = jnp.dot(turned[...], window, preferred_element_type=F32)
            for c in range(3):
                kgp[t, a * 3 + c] = part[c * pair:(c + 1) * pair]
            return 0

        lax.fori_loop(0, 3, tap_row, 0)
        mate_part(t).start()
        if t:
            pair_sum(t - 1)
        if t == 1:
            @pl.when(jnp.logical_not(inner))
            def _():
                z_part(0, beside, 0).start()
        if t == 3:
            @pl.when(inner)
            def _():
                z_part(2, beside, 2).start()
    pair_sum(3)

    def keep(i, _):
        kg_ref[i] = kgp[3, i, mine]
        return 0

    lax.fori_loop(0, taps, keep, 0)
    neighbours(1)

    def weights_pass(t, k):
        rows = lanes(peer(t, k), ch)
        return remote(wb.at[:, rows], wb.at[:, rows], wq_send.at[t], wq_recv.at[t], row, mate)

    def convolve(grid_ref, weights, dims, flip, result, n):
        def image(b, _):
            sums = []
            for c in range(3):
                total = None
                for a in range(3):
                    block = grid_ref[b, pl.ds(2 - a if flip else a, height)].reshape(height * width, grid_ref.shape[3])
                    part = lax.dot_general(block, weights[a * 3 + c], (dims, ((), ())), preferred_element_type=F32)
                    total = part if total is None else total + part
                sums.append(total)
            if flip:
                sums = sums[::-1]
            value = shift_sum(*sums, width).astype(BF16).reshape(height, width, pair)

            @pl.when(core == 0)
            def _():
                result[b] = value[:, :, :ch]
                stage[n, b] = value[:, :, ch:]

            @pl.when(core == 1)
            def _():
                result[half + b] = value[:, :, ch:]
                stage[n, b] = value[:, :, :ch]

            return 0

        lax.fori_loop(0, half, image, 0)

    def result_mate(n, result, batch_half):
        return remote(
            stage.at[n], result.at[pl.ds(batch_half * half, half)], op_send.at[n], op_recv.at[n], row, mate
        )

    weights_mate(1).wait_recv()
    convolve(xg, wf, ((1,), (1,)), False, out_ref, 0)
    result_mate(0, out_ref, core).start()

    @pl.when(inner)
    def _():
        relay(0)

    @pl.when(jnp.logical_not(inner))
    def _():
        z_part(1, beside, 1).start()

    wb_own.wait()
    weights_pass(0, 0).start()
    for t in range(1, 4):
        weights_c(t, peer(t, 0)).wait_recv()
        weights_pass(t, 0).start()
    passed(1, 0).wait_recv()
    passed(1, 1).wait_recv()
    for t in range(4):
        weights_pass(t, 1).wait_recv()

    @pl.when(inner)
    def _():
        relay(1)

    @pl.when(jnp.logical_not(inner))
    def _():
        z_part(2, beside, 2).start()

    convolve(gg, wb, ((1,), (0,)), True, ig_ref, 1)
    result_mate(1, ig_ref, core).start()

    for slot in (2, 3):
        z_part(0, beside, slot).wait_recv()

        def add(i, _):
            kg_ref[i] = kg_ref[i] + kgz[slot, i]
            return 0

        lax.fori_loop(0, taps, add, 0)

    for n in range(2):
        for t, k in peers:
            body_copy(n, t, k, col).wait_send()
        for side in range(2):
            @pl.when(has(1 - side))
            def _():
                halo_z(n, side).wait_send()

            @pl.when(has(side))
            def _():
                for t, k in peers:
                    halo_c(n, side, t, k, col).wait_send()
        for side in range(2):
            pass_on(n, side).wait_send()
    weights_own(0, beside).wait_send()

    @pl.when(inner)
    def _():
        for index in range(1, 5):
            weights_own(index, beside).wait_send()

    weights_mate(0).wait_send()
    for t in range(1, 4):
        weights_c(t, col).wait_send()
    for t in range(4):
        weights_pass(t, 0).wait_send()
        mate_part(t).wait_send()
        if t < 3:
            z_part(t, beside, t).wait_send()

    result_mate(0, out_ref, core).wait_send()
    result_mate(1, ig_ref, core).wait_send()
    result_mate(0, out_ref, 1 - core).wait_recv()
    result_mate(1, ig_ref, 1 - core).wait_recv()


def fused(images, upstream, weights):
    n_row, n_col = lax.axis_size("row"), lax.axis_size("col")
    batch, height, width, ch = images.shape
    taps, pair, half = weights.shape[0], 2 * ch, batch // 2
    every = ch * n_col
    dma = pltpu.SemaphoreType.DMA
    vmem = pl.BlockSpec(memory_space=pltpu.VMEM)
    grid = (half, height + 2, width, every)
    flops = 3 * 2 * half * height * width * every * pair * taps
    return pl.pallas_call(
        functools.partial(kernel, n_row),
        out_shape=(
            jax.ShapeDtypeStruct(images.shape, BF16),
            jax.ShapeDtypeStruct(images.shape, BF16),
            jax.ShapeDtypeStruct(weights.shape, F32),
        ),
        in_specs=[vmem] * 3,
        out_specs=(vmem,) * 3,
        scratch_shapes=[
            pltpu.VMEM(grid, BF16),
            pltpu.VMEM(grid, BF16),
            pltpu.VMEM((taps, pair, every), BF16),
            pltpu.VMEM((taps, every, pair), BF16),
            pltpu.VMEM((2, 2, batch, 1, width, ch), BF16),
            pltpu.VMEM((3 * pair, half * height * width), BF16),
            pltpu.VMEM((4, taps, pair, pair), F32),
            pltpu.VMEM((4, taps, ch, pair), F32),
            pltpu.VMEM((n_row, taps, ch, pair), F32),
            pltpu.VMEM((2, half, height, width, ch), BF16),
            dma((4,)),
            dma((2, 4, 2)), dma((2, 4, 2)),
            dma((2, 2)), dma((2, 2)),
            dma((2, 2)), dma((2, 2)),
            dma((2, 2, 4, 2)), dma((2, 2, 4, 2)),
            dma((5,)), dma((n_row,)),
            dma, dma,
            dma((4,)), dma((4,)),
            dma((4,)), dma((4,)),
            dma((4,)), dma((4,)),
            dma((4,)), dma((n_row,)),
            dma((2,)), dma((2,)),
        ],
        compiler_params=pltpu.CompilerParams(
            collective_id=0, has_side_effects=True, vmem_limit_bytes=60 * 1024 * 1024
        ),
        cost_estimate=pl.CostEstimate(flops=flops, bytes_accessed=8 * 1024 * 1024, transcendentals=0),
    )(images, upstream, weights)


def fits(n_row, n_col, images, kernel_block):
    ch = images.shape[2] // W
    return (
        n_row == 4 and n_col == 8 and ch == 128 and images.shape[0] % 4 == 0
        and kernel_block.shape[2] == ch and kernel_block.shape[3] == 2 * ch and images.size <= 8 * 8 * 8192
    )


def to_last(flat):
    return to_maps(flat).transpose(0, 1, 3, 2)


def from_last(maps):
    return to_flat(maps.transpose(0, 1, 3, 2))


def padded_2(block, sides, width):
    for axis, dim in sides:
        count = lax.axis_size(axis)
        forward = [(i, i + 1) for i in range(count - 1)]
        backward = [(target, source) for source, target in forward]
        low = lax.ppermute(
            lax.slice_in_dim(block, block.shape[dim] - width, None, axis=dim), axis, forward
        )
        high = lax.ppermute(lax.slice_in_dim(block, 0, width, axis=dim), axis, backward)
        block = jnp.concatenate([low, block, high], axis=dim)
    return block


def convolve_valid(inputs, weights, weight_spec):
    return lax.conv_general_dilated(
        inputs,
        weights,
        (1, 1),
        ((0, 0), (1, 1)),
        dimension_numbers=("NHCW", weight_spec, "NHCW"),
        preferred_element_type=jnp.float32,
    )


def to_maps(flat):
    return flat.reshape(flat.shape[0], flat.shape[1], flat.shape[2] // W, W)


def to_flat(maps):
    return maps.reshape(maps.shape[0], maps.shape[1], maps.shape[2] * maps.shape[3])


def gathered(images, kernel, upstream):
    weights_all = lax.all_gather(kernel, "row", axis=3, tiled=True)
    images_rim = padded_2(images, (("row", 1),), 1)
    grads_rim = padded_2(upstream, (("row", 1),), 1)
    grads_maps = to_maps(grads_rim)
    batch = images.shape[0]
    height = images.shape[1]
    width = W
    out_local = kernel.shape[2]
    grads_mid = grads_maps[:, 1:-1]
    output_init = jnp.zeros((batch, height, out_local, width), jnp.float32)
    output_sum = output_init
    panel_in = to_maps(lax.all_gather(images_rim, "col", axis=2, tiled=True))
    count_here = panel_in.shape[2]
    output_sum = output_sum + convolve_valid(panel_in, weights_all, "HWOI")
    padded = jnp.pad(panel_in, ((0, 0), (0, 0), (0, 0), (1, 1)))
    blocks = []
    for tap_row in range(3):
        for tap_col in range(3):
            window = padded[:, tap_row : tap_row + height, :, tap_col : tap_col + width]
            blocks.append(
                jnp.einsum("bhiw,bhow->oi", window, grads_mid, preferred_element_type=jnp.float32)
            )
    stacked = jnp.stack(blocks).reshape(3, 3, out_local, count_here)
    output_sum, weight_part = (output_sum, stacked)
    kernel_grad = lax.psum_scatter(weight_part, "row", scatter_dimension=3, tiled=True)
    flipped = jnp.flip(weights_all, (0, 1))
    partial_grad = to_flat(convolve_valid(grads_maps, flipped, "HWIO"))
    input_grad = lax.psum_scatter(partial_grad, "col", scatter_dimension=2, tiled=True)
    return (to_flat(output_sum).astype(jnp.bfloat16), input_grad.astype(jnp.bfloat16), kernel_grad)


def shards(images, kernel_block, upstream):
    if not fits(lax.axis_size("row"), lax.axis_size("col"), images, kernel_block):
        return gathered(images, kernel_block, upstream)
    taps = kernel_block.reshape((9,) + kernel_block.shape[2:])
    out, grad, kernel_grad = fused(to_last(images), to_last(upstream), taps)
    return from_last(out), from_last(grad), kernel_grad.reshape(kernel_block.shape)


def solution(mesh):
    return jax.shard_map(
        shards,
        mesh=mesh,
        in_specs=(P(None, "row", "col"), P(None, None, "col", "row"), P(None, "row", "col")),
        out_specs=(P(None, "row", "col"), P(None, "row", "col"), P(None, None, "col", "row")),
        check_vma=False,
    )
```

```python
import functools

import jax
import jax.numpy as jnp
from jax import lax
from jax.experimental import pallas as pl
from jax.experimental.pallas import tpu as pltpu
from jax.sharding import PartitionSpec as P

W = 64
MESH = pl.DeviceIdType.MESH
F32 = jnp.float32
BF16 = jnp.bfloat16


def remote(src, dst, send, recv, row, col):
    return pltpu.make_async_remote_copy(
        src_ref=src, dst_ref=dst, send_sem=send, recv_sem=recv, device_id=(row, col), device_id_type=MESH
    )


def shift_sum(low, mid, high, width):
    rows = low.shape[0]
    at = lax.rem(lax.broadcasted_iota(jnp.int32, low.shape, 0), jnp.int32(width))
    first = jnp.where(at == 0, 0.0, pltpu.roll(low, 1, 0))
    last = jnp.where(at == width - 1, 0.0, pltpu.roll(high, rows - 1, 0))
    return first + mid + last


def kernel(
    n_row, x_ref, g_ref, w_ref, out_ref, ig_ref, kg_ref,
    xg, gg, wf, wb, halo, turned, kgp, kgr, kgz, stage, held,
    own_sem, ax_send, ax_recv, fx_send, fx_recv, hz_send, hz_recv, hc_send, hc_recv,
    wz_send, wz_recv, wp_send, wp_recv, wc_send, wc_recv, wq_send, wq_recv,
    kp_send, kp_recv, kz_send, kz_recv, op_send, op_recv,
):
    batch, height, width, ch = x_ref.shape
    half = batch // 2
    pair = 2 * ch
    taps = w_ref.shape[0]
    row, col = lax.axis_index("row"), lax.axis_index("col")
    chip, core = col // 2, lax.rem(col, 2)
    mate = chip * 2 + 1 - core

    def chip_at(t):
        cx, cy = lax.rem(chip, 2), chip // 2
        return lax.rem(cy + t // 2, 2) * 2 + lax.rem(cx + t % 2, 2)

    chips = [chip_at(t) for t in range(4)]
    every_peer = [(t, k) for t in range(4) for k in range(2) if (t, k) != (0, 0)]
    peers = [(t, k) for t, k in every_peer if t < 3]

    def peer(t, k):
        return chips[t] * 2 + lax.rem(core + k, 2)

    def row_at(s):
        return lax.rem(row + s, n_row)

    barrier = pltpu.get_barrier_semaphore()
    for t, k in every_peer:
        pl.semaphore_signal(barrier, inc=1, device_id=(row, peer(t, k)), device_id_type=MESH)
    for s in range(1, n_row):
        pl.semaphore_signal(barrier, inc=1, device_id=(row_at(s), col), device_id_type=MESH)
    pl.semaphore_wait(barrier, len(every_peer) + n_row - 1)

    def lanes(c, size):
        return pl.ds(pl.multiple_of(c * size, size), size)

    own = pl.ds(core * half, half)
    arrays = ((x_ref, xg), (g_ref, gg))
    has_up, has_down = row > 0, row < n_row - 1

    def body_copy(n, t, k, source):
        src, dst = arrays[n]
        to = peer(t, k)
        return remote(
            src.at[pl.ds(lax.rem(core + k, 2) * half, half)],
            dst.at[:, pl.ds(1, height), :, lanes(source, ch)],
            ax_send.at[n, t, k], ax_recv.at[n, t, k], row, to,
        )

    def halo_z(n, side):
        src, _ = arrays[n]
        at = height - 1 if side == 0 else 0
        to = row + 1 if side == 0 else row - 1
        return remote(src.at[:, pl.ds(at, 1)], halo.at[n, side], hz_send.at[n, side], hz_recv.at[n, side], to, col)

    def halo_c(n, side, t, k, source):
        _, dst = arrays[n]
        at = 0 if side == 0 else height + 1
        return remote(
            halo.at[n, side, pl.ds(lax.rem(core + k, 2) * half, half)],
            dst.at[:, pl.ds(at, 1), :, lanes(source, ch)],
            hc_send.at[n, side, t, k], hc_recv.at[n, side, t, k], row, peer(t, k),
        )

    def halo_own(n, side):
        _, dst = arrays[n]
        at = 0 if side == 0 else height + 1
        return pltpu.make_async_copy(
            halo.at[n, side, own], dst.at[:, pl.ds(at, 1), :, lanes(col, ch)], hc_send.at[n, side, 0, 0]
        )

    half_z = row // 2
    inner = (row == 1) | (row == 2)
    beside = row + 1 - 2 * lax.rem(row, 2)
    across = 2 - half_z
    far = 3 * (1 - half_z)
    blocks = [far, across, beside, row]

    def weights_z(source, index, to):
        part = wf.at[:, lanes(core, ch), lanes(source, pair)]
        return remote(part, part, wz_send.at[index], wz_recv.at[source], to, col)

    def weights_own(index, to):
        part = wf.at[:, lanes(core, ch), lanes(row, pair)]
        return remote(w_ref, part, wz_send.at[index], wz_recv.at[row], to, col)

    def pass_on(n, side):
        _, dst = arrays[n]
        part = dst.at[pl.ds(side * (half // 2), half // 2), :, :, lanes(chips[1 + side], pair)]
        return remote(part, part, fx_send.at[n, side], fx_recv.at[n, side], row, peer(2 - side, 0))

    def passed(n, side):
        _, dst = arrays[n]
        part = dst.at[pl.ds(side * (half // 2), half // 2), :, :, lanes(chips[3], pair)]
        return remote(part, part, fx_send.at[n, side], fx_recv.at[n, side], row, peer(2 - side, 0))

    def has(side):
        return has_up if side == 0 else has_down

    @pl.when(has_down)
    def _():
        for n in range(2):
            halo_z(n, 0).start()

    @pl.when(has_up)
    def _():
        for n in range(2):
            halo_z(n, 1).start()

    own_copies = [
        pltpu.make_async_copy(x_ref.at[own], xg.at[:, pl.ds(1, height), :, lanes(col, ch)], own_sem.at[0]),
        pltpu.make_async_copy(g_ref.at[own], gg.at[:, pl.ds(1, height), :, lanes(col, ch)], own_sem.at[1]),
        pltpu.make_async_copy(w_ref, wf.at[:, lanes(core, ch), lanes(row, pair)], own_sem.at[2]),
    ]
    for copy in own_copies:
        copy.start()
    body_copy(1, 0, 1, col).start()
    for t, k in peers:
        body_copy(0, t, k, col).start()
    weights_own(0, beside).start()

    @pl.when(inner)
    def _():
        weights_own(1, across).start()

    def clear(at):
        for t in range(3):
            for grid_ref in (xg, gg):
                grid_ref[:, at, :, lanes(chips[t], pair)] = jnp.zeros((half, width, pair), BF16)

    @pl.when(jnp.logical_not(has_up))
    def _():
        clear(0)

    @pl.when(jnp.logical_not(has_down))
    def _():
        clear(height + 1)

    def spread_halo(n):
        for side in range(2):
            @pl.when(has(side))
            def _():
                halo_z(n, side).wait_recv()
                halo_own(n, side).start()
                for t, k in peers:
                    halo_c(n, side, t, k, col).start()

    spread_halo(0)

    own_copies[0].wait()
    own_copies[1].wait()
    body_copy(1, 0, 1, mate).wait_recv()

    def turn(b, _):
        block = gg[b, pl.ds(1, height), :, lanes(chip, pair)].astype(F32).reshape(height * width, pair)
        at = lax.rem(lax.broadcasted_iota(jnp.int32, block.shape, 0), jnp.int32(width))
        rows = height * width
        left = jnp.where(at == width - 1, 0.0, pltpu.roll(block, rows - 1, 0))
        right = jnp.where(at == 0, 0.0, pltpu.roll(block, 1, 0))
        where = pl.ds(pl.multiple_of(b * rows, rows), rows)
        for c, part in enumerate((left, block, right)):
            turned[c * pair:(c + 1) * pair, where] = part.T.astype(BF16)
        return 0

    lax.fori_loop(0, half, turn, 0)

    def wait_halos(n, t):
        for side in range(2):
            @pl.when(has(side))
            def _():
                for k in range(2):
                    if (t, k) == (0, 0):
                        halo_own(n, side).wait()
                    else:
                        halo_c(n, side, t, k, peer(t, k)).wait_recv()

    def mate_part(t):
        theirs = pl.ds(pl.multiple_of((1 - core) * ch, ch), ch)
        return remote(kgp.at[t, :, theirs], kgr.at[t], kp_send.at[t], kp_recv.at[t], row, mate)

    mine = pl.ds(pl.multiple_of(core * ch, ch), ch)

    def z_part(t, to, slot):
        return remote(kgp.at[t, :, mine], kgz.at[slot], kz_send.at[t], kz_recv.at[slot], to, col)

    def add_in(t, other):
        def add(i, _):
            kgp[t, i, mine] = kgp[t, i, mine] + other[i]
            return 0

        lax.fori_loop(0, taps, add, 0)

    def pair_sum(t):
        mate_part(t).wait_recv()
        add_in(t, kgr.at[t])

    def relay(t):
        z_part(t, beside, t).wait_recv()
        add_in(t, kgz.at[t])
        z_part(t, blocks[t], 3).start()

    own_copies[2].wait()

    @pl.when(inner)
    def _():
        weights_z(beside, 2, across).wait_recv()
        weights_z(beside, 2, across).start()
        weights_z(across, 3, beside).wait_recv()
        weights_z(across, 3, beside).start()

    def neighbours(n):
        for t in range(3):
            for k in range(2):
                if t:
                    body_copy(n, t, k, peer(t, k)).wait_recv()
            wait_halos(n, t)
            if t:
                pass_on(n, t - 1).start()

    neighbours(0)
    for t, k in peers:
        if t:
            body_copy(1, t, k, col).start()
    spread_halo(1)

    @pl.when(inner)
    def _():
        weights_z(far, 4, beside).wait_recv()
        weights_z(far, 4, beside).start()

    @pl.when(jnp.logical_not(inner))
    def _():
        for source in (beside, across, far):
            weights_z(source, 0, beside).wait_recv()

    def weights_mate(k):
        mine = lanes(core if k == 0 else 1 - core, ch)
        return remote(wf.at[:, mine], wf.at[:, mine], wp_send, wp_recv, row, mate)

    def weights_c(t, source):
        return remote(
            wf.at[:, lanes(core, ch), lanes(chips[t], pair)], wb.at[:, lanes(source, ch)],
            wc_send.at[t], wc_recv.at[t], row, peer(t, 0),
        )

    weights_mate(0).start()
    wb_own = pltpu.make_async_copy(wf.at[:, lanes(core, ch), lanes(chip, pair)], wb.at[:, lanes(col, ch)], own_sem.at[3])
    wb_own.start()
    for t in range(1, 4):
        weights_c(t, col).start()
    body_copy(0, 0, 1, mate).wait_recv()
    passed(0, 0).wait_recv()
    passed(0, 1).wait_recv()

    for t in range(4):
        def tap_row(a, _):
            window = xg[:, pl.ds(a, height), :, lanes(blocks[t], pair)].reshape(half * height * width, pair)
            part = jnp.dot(turned[...], window, preferred_element_type=F32)
            for c in range(3):
                kgp[t, a * 3 + c] = part[c * pair:(c + 1) * pair]
            return 0

        lax.fori_loop(0, 3, tap_row, 0)
        mate_part(t).start()
        if t:
            pair_sum(t - 1)
        if t == 1:
            @pl.when(jnp.logical_not(inner))
            def _():
                z_part(0, beside, 0).start()
        if t == 3:
            @pl.when(inner)
            def _():
                z_part(2, beside, 2).start()
    pair_sum(3)

    def keep(i, _):
        kg_ref[i] = kgp[3, i, mine]
        return 0

    lax.fori_loop(0, taps, keep, 0)
    neighbours(1)

    def weights_pass(t, k):
        rows = lanes(peer(t, k), ch)
        return remote(wb.at[:, rows], wb.at[:, rows], wq_send.at[t], wq_recv.at[t], row, mate)

    def result_mate(n, result, batch_half, b):
        return remote(
            stage.at[n, b], result.at[batch_half * half + b], op_send.at[n, b], op_recv.at[n, b], row, mate
        )

    def convolve(grid_ref, weights, dims, flip, result, n, parts, start, finish):
        def image(b, _):
            sums = []
            for c in range(3):
                total = None
                for a in range(3):
                    for t in parts:
                        at = slice(None) if t is None else lanes(chips[t], pair)
                        block = grid_ref[b, pl.ds(2 - a if flip else a, height), :, at]
                        block = block.reshape(height * width, block.shape[2])
                        tap = weights[a * 3 + c] if t is None else weights[a * 3 + c, at]
                        part = lax.dot_general(block, tap, (dims, ((), ())), preferred_element_type=F32)
                        total = part if total is None else total + part
                sums.append(total)
            if flip:
                sums = sums[::-1]
            value = shift_sum(*sums, width)
            if not start:
                value = value + held[b]
            if not finish:
                held[b] = value
                return 0
            value = value.astype(BF16).reshape(height, width, pair)

            @pl.when(core == 0)
            def _():
                result[b] = value[:, :, :ch]
                stage[n, b] = value[:, :, ch:]

            @pl.when(core == 1)
            def _():
                result[half + b] = value[:, :, ch:]
                stage[n, b] = value[:, :, :ch]

            result_mate(n, result, core, b).start()
            return 0

        lax.fori_loop(0, half, image, 0)

    weights_mate(1).wait_recv()
    convolve(xg, wf, ((1,), (1,)), False, out_ref, 0, (None,), True, True)

    @pl.when(inner)
    def _():
        relay(0)

    @pl.when(jnp.logical_not(inner))
    def _():
        z_part(1, beside, 1).start()

    wb_own.wait()
    weights_pass(0, 0).start()
    for t in range(1, 3):
        weights_c(t, peer(t, 0)).wait_recv()
        weights_pass(t, 0).start()
    for t in range(3):
        weights_pass(t, 1).wait_recv()
    convolve(gg, wb, ((1,), (0,)), True, ig_ref, 1, (0, 1, 2), True, False)
    weights_c(3, peer(3, 0)).wait_recv()
    weights_pass(3, 0).start()

    @pl.when(inner)
    def _():
        relay(1)

    @pl.when(jnp.logical_not(inner))
    def _():
        z_part(1, beside, 1).wait_send()
        z_part(2, beside, 2).start()

    passed(1, 0).wait_recv()
    passed(1, 1).wait_recv()
    weights_pass(3, 1).wait_recv()
    convolve(gg, wb, ((1,), (0,)), True, ig_ref, 1, (3,), False, True)

    for slot in (2, 3):
        z_part(0, beside, slot).wait_recv()

        def add(i, _):
            kg_ref[i] = kg_ref[i] + kgz[slot, i]
            return 0

        lax.fori_loop(0, taps, add, 0)

    for n in range(2):
        for t, k in peers:
            body_copy(n, t, k, col).wait_send()
        for side in range(2):
            @pl.when(has(1 - side))
            def _():
                halo_z(n, side).wait_send()

            @pl.when(has(side))
            def _():
                for t, k in peers:
                    halo_c(n, side, t, k, col).wait_send()
        for side in range(2):
            pass_on(n, side).wait_send()
    weights_own(0, beside).wait_send()

    @pl.when(inner)
    def _():
        for index in range(1, 5):
            weights_own(index, beside).wait_send()

    weights_mate(0).wait_send()
    for t in range(1, 4):
        weights_c(t, col).wait_send()
    for t in range(4):
        weights_pass(t, 0).wait_send()
        mate_part(t).wait_send()
        if t in (0, 2):
            z_part(t, beside, t).wait_send()

    @pl.when(inner)
    def _():
        z_part(1, beside, 1).wait_send()

    def settle(b, _):
        for n, result in enumerate((out_ref, ig_ref)):
            result_mate(n, result, core, b).wait_send()
            result_mate(n, result, 1 - core, b).wait_recv()
        return 0

    lax.fori_loop(0, half, settle, 0)


def fused(images, upstream, weights):
    n_row, n_col = lax.axis_size("row"), lax.axis_size("col")
    batch, height, width, ch = images.shape
    taps, pair, half = weights.shape[0], 2 * ch, batch // 2
    every = ch * n_col
    dma = pltpu.SemaphoreType.DMA
    vmem = pl.BlockSpec(memory_space=pltpu.VMEM)
    grid = (half, height + 2, width, every)
    flops = 3 * 2 * half * height * width * every * pair * taps
    return pl.pallas_call(
        functools.partial(kernel, n_row),
        out_shape=(
            jax.ShapeDtypeStruct(images.shape, BF16),
            jax.ShapeDtypeStruct(images.shape, BF16),
            jax.ShapeDtypeStruct(weights.shape, F32),
        ),
        in_specs=[vmem] * 3,
        out_specs=(vmem,) * 3,
        scratch_shapes=[
            pltpu.VMEM(grid, BF16),
            pltpu.VMEM(grid, BF16),
            pltpu.VMEM((taps, pair, every), BF16),
            pltpu.VMEM((taps, every, pair), BF16),
            pltpu.VMEM((2, 2, batch, 1, width, ch), BF16),
            pltpu.VMEM((3 * pair, half * height * width), BF16),
            pltpu.VMEM((4, taps, pair, pair), F32),
            pltpu.VMEM((4, taps, ch, pair), F32),
            pltpu.VMEM((n_row, taps, ch, pair), F32),
            pltpu.VMEM((2, half, height, width, ch), BF16),
            pltpu.VMEM((half, height * width, pair), F32),
            dma((4,)),
            dma((2, 4, 2)), dma((2, 4, 2)),
            dma((2, 2)), dma((2, 2)),
            dma((2, 2)), dma((2, 2)),
            dma((2, 2, 4, 2)), dma((2, 2, 4, 2)),
            dma((5,)), dma((n_row,)),
            dma, dma,
            dma((4,)), dma((4,)),
            dma((4,)), dma((4,)),
            dma((4,)), dma((4,)),
            dma((4,)), dma((n_row,)),
            dma((2, half)), dma((2, half)),
        ],
        compiler_params=pltpu.CompilerParams(
            collective_id=0, has_side_effects=True, vmem_limit_bytes=60 * 1024 * 1024
        ),
        cost_estimate=pl.CostEstimate(flops=flops, bytes_accessed=8 * 1024 * 1024, transcendentals=0),
    )(images, upstream, weights)


def fits(n_row, n_col, images, kernel_block):
    ch = images.shape[2] // W
    return (
        n_row == 4 and n_col == 8 and ch == 128 and images.shape[0] % 4 == 0
        and kernel_block.shape[2] == ch and kernel_block.shape[3] == 2 * ch and images.size <= 8 * 8 * 8192
    )


def to_last(flat):
    return to_maps(flat).transpose(0, 1, 3, 2)


def from_last(maps):
    return to_flat(maps.transpose(0, 1, 3, 2))


def padded_2(block, sides, width):
    for axis, dim in sides:
        count = lax.axis_size(axis)
        forward = [(i, i + 1) for i in range(count - 1)]
        backward = [(target, source) for source, target in forward]
        low = lax.ppermute(
            lax.slice_in_dim(block, block.shape[dim] - width, None, axis=dim), axis, forward
        )
        high = lax.ppermute(lax.slice_in_dim(block, 0, width, axis=dim), axis, backward)
        block = jnp.concatenate([low, block, high], axis=dim)
    return block


def convolve_valid(inputs, weights, weight_spec):
    return lax.conv_general_dilated(
        inputs,
        weights,
        (1, 1),
        ((0, 0), (1, 1)),
        dimension_numbers=("NHCW", weight_spec, "NHCW"),
        preferred_element_type=jnp.float32,
    )


def to_maps(flat):
    return flat.reshape(flat.shape[0], flat.shape[1], flat.shape[2] // W, W)


def to_flat(maps):
    return maps.reshape(maps.shape[0], maps.shape[1], maps.shape[2] * maps.shape[3])


def gathered(images, kernel, upstream):
    weights_all = lax.all_gather(kernel, "row", axis=3, tiled=True)
    images_rim = padded_2(images, (("row", 1),), 1)
    grads_rim = padded_2(upstream, (("row", 1),), 1)
    grads_maps = to_maps(grads_rim)
    batch = images.shape[0]
    height = images.shape[1]
    width = W
    out_local = kernel.shape[2]
    grads_mid = grads_maps[:, 1:-1]
    output_init = jnp.zeros((batch, height, out_local, width), jnp.float32)
    output_sum = output_init
    panel_in = to_maps(lax.all_gather(images_rim, "col", axis=2, tiled=True))
    count_here = panel_in.shape[2]
    output_sum = output_sum + convolve_valid(panel_in, weights_all, "HWOI")
    padded = jnp.pad(panel_in, ((0, 0), (0, 0), (0, 0), (1, 1)))
    blocks = []
    for tap_row in range(3):
        for tap_col in range(3):
            window = padded[:, tap_row : tap_row + height, :, tap_col : tap_col + width]
            blocks.append(
                jnp.einsum("bhiw,bhow->oi", window, grads_mid, preferred_element_type=jnp.float32)
            )
    stacked = jnp.stack(blocks).reshape(3, 3, out_local, count_here)
    output_sum, weight_part = (output_sum, stacked)
    kernel_grad = lax.psum_scatter(weight_part, "row", scatter_dimension=3, tiled=True)
    flipped = jnp.flip(weights_all, (0, 1))
    partial_grad = to_flat(convolve_valid(grads_maps, flipped, "HWIO"))
    input_grad = lax.psum_scatter(partial_grad, "col", scatter_dimension=2, tiled=True)
    return (to_flat(output_sum).astype(jnp.bfloat16), input_grad.astype(jnp.bfloat16), kernel_grad)


def shards(images, kernel_block, upstream):
    if not fits(lax.axis_size("row"), lax.axis_size("col"), images, kernel_block):
        return gathered(images, kernel_block, upstream)
    taps = kernel_block.reshape((9,) + kernel_block.shape[2:])
    out, grad, kernel_grad = fused(to_last(images), to_last(upstream), taps)
    return from_last(out), from_last(grad), kernel_grad.reshape(kernel_block.shape)


def solution(mesh):
    return jax.shard_map(
        shards,
        mesh=mesh,
        in_specs=(P(None, "row", "col"), P(None, None, "col", "row"), P(None, "row", "col")),
        out_specs=(P(None, "row", "col"), P(None, "row", "col"), P(None, None, "col", "row")),
        check_vma=False,
    )
```

```python
import functools

import jax
import jax.numpy as jnp
from jax import lax
from jax.experimental import pallas as pl
from jax.experimental.pallas import tpu as pltpu
from jax.sharding import PartitionSpec as P

W = 64
MESH = pl.DeviceIdType.MESH
F32 = jnp.float32
BF16 = jnp.bfloat16


def remote(src, dst, send, recv, row, col):
    return pltpu.make_async_remote_copy(
        src_ref=src, dst_ref=dst, send_sem=send, recv_sem=recv, device_id=(row, col), device_id_type=MESH
    )


def shift_sum(low, mid, high, width):
    rows = low.shape[0]
    at = lax.rem(lax.broadcasted_iota(jnp.int32, low.shape, 0), jnp.int32(width))
    first = jnp.where(at == 0, 0.0, pltpu.roll(low, 1, 0))
    last = jnp.where(at == width - 1, 0.0, pltpu.roll(high, rows - 1, 0))
    return first + mid + last


def kernel(
    n_row, x_ref, g_ref, w_ref, out_ref, ig_ref, kg_ref,
    xg, gg, wf, wb, halo, turned, kgp, kgr, kgz, stage, held,
    own_sem, ax_send, ax_recv, fx_send, fx_recv, hz_send, hz_recv, hc_send, hc_recv,
    wz_send, wz_recv, wp_send, wp_recv, wc_send, wc_recv, wq_send, wq_recv,
    kp_send, kp_recv, kz_send, kz_recv, op_send, op_recv,
):
    batch, height, width, ch = x_ref.shape
    half = batch // 2
    pair = 2 * ch
    taps = w_ref.shape[0]
    row, col = lax.axis_index("row"), lax.axis_index("col")
    chip, core = col // 2, lax.rem(col, 2)
    mate = chip * 2 + 1 - core

    def chip_at(t):
        cx, cy = lax.rem(chip, 2), chip // 2
        return lax.rem(cy + t // 2, 2) * 2 + lax.rem(cx + t % 2, 2)

    chips = [chip_at(t) for t in range(4)]
    every_peer = [(t, k) for t in range(4) for k in range(2) if (t, k) != (0, 0)]
    peers = [(t, k) for t, k in every_peer if t < 3]

    def peer(t, k):
        return chips[t] * 2 + lax.rem(core + k, 2)

    def row_at(s):
        return lax.rem(row + s, n_row)

    barrier = pltpu.get_barrier_semaphore()
    for t, k in every_peer:
        pl.semaphore_signal(barrier, inc=1, device_id=(row, peer(t, k)), device_id_type=MESH)
    for s in range(1, n_row):
        pl.semaphore_signal(barrier, inc=1, device_id=(row_at(s), col), device_id_type=MESH)
    pl.semaphore_wait(barrier, len(every_peer) + n_row - 1)

    def lanes(c, size):
        return pl.ds(pl.multiple_of(c * size, size), size)

    own = pl.ds(core * half, half)
    arrays = ((x_ref, xg), (g_ref, gg))
    has_up, has_down = row > 0, row < n_row - 1

    def body_copy(n, t, k, source):
        src, dst = arrays[n]
        to = peer(t, k)
        return remote(
            src.at[pl.ds(lax.rem(core + k, 2) * half, half)],
            dst.at[:, pl.ds(1, height), :, lanes(source, ch)],
            ax_send.at[n, t, k], ax_recv.at[n, t, k], row, to,
        )

    def halo_z(n, side):
        src, _ = arrays[n]
        at = height - 1 if side == 0 else 0
        to = row + 1 if side == 0 else row - 1
        return remote(src.at[:, pl.ds(at, 1)], halo.at[n, side], hz_send.at[n, side], hz_recv.at[n, side], to, col)

    def halo_c(n, side, t, k, source):
        _, dst = arrays[n]
        at = 0 if side == 0 else height + 1
        return remote(
            halo.at[n, side, pl.ds(lax.rem(core + k, 2) * half, half)],
            dst.at[:, pl.ds(at, 1), :, lanes(source, ch)],
            hc_send.at[n, side, t, k], hc_recv.at[n, side, t, k], row, peer(t, k),
        )

    def halo_own(n, side):
        _, dst = arrays[n]
        at = 0 if side == 0 else height + 1
        return pltpu.make_async_copy(
            halo.at[n, side, own], dst.at[:, pl.ds(at, 1), :, lanes(col, ch)], hc_send.at[n, side, 0, 0]
        )

    half_z = row // 2
    inner = (row == 1) | (row == 2)
    beside = row + 1 - 2 * lax.rem(row, 2)
    across = 2 - half_z
    far = 3 * (1 - half_z)
    blocks = [far, across, beside, row]

    def weights_z(source, index, to):
        part = wf.at[:, lanes(core, ch), lanes(source, pair)]
        return remote(part, part, wz_send.at[index], wz_recv.at[source], to, col)

    def weights_own(index, to):
        part = wf.at[:, lanes(core, ch), lanes(row, pair)]
        return remote(w_ref, part, wz_send.at[index], wz_recv.at[row], to, col)

    def pass_on(n, side):
        _, dst = arrays[n]
        part = dst.at[pl.ds(side * (half // 2), half // 2), :, :, lanes(chips[1 + side], pair)]
        return remote(part, part, fx_send.at[n, side], fx_recv.at[n, side], row, peer(2 - side, 0))

    def passed(n, side):
        _, dst = arrays[n]
        part = dst.at[pl.ds(side * (half // 2), half // 2), :, :, lanes(chips[3], pair)]
        return remote(part, part, fx_send.at[n, side], fx_recv.at[n, side], row, peer(2 - side, 0))

    def has(side):
        return has_up if side == 0 else has_down

    @pl.when(has_down)
    def _():
        for n in range(2):
            halo_z(n, 0).start()

    @pl.when(has_up)
    def _():
        for n in range(2):
            halo_z(n, 1).start()

    own_copies = [
        pltpu.make_async_copy(x_ref.at[own], xg.at[:, pl.ds(1, height), :, lanes(col, ch)], own_sem.at[0]),
        pltpu.make_async_copy(g_ref.at[own], gg.at[:, pl.ds(1, height), :, lanes(col, ch)], own_sem.at[1]),
        pltpu.make_async_copy(w_ref, wf.at[:, lanes(core, ch), lanes(row, pair)], own_sem.at[2]),
    ]
    for copy in own_copies:
        copy.start()
    body_copy(1, 0, 1, col).start()
    for t, k in peers:
        body_copy(0, t, k, col).start()
    weights_own(0, beside).start()

    @pl.when(inner)
    def _():
        weights_own(1, across).start()

    def clear(at):
        for t in range(3):
            for grid_ref in (xg, gg):
                grid_ref[:, at, :, lanes(chips[t], pair)] = jnp.zeros((half, width, pair), BF16)

    @pl.when(jnp.logical_not(has_up))
    def _():
        clear(0)

    @pl.when(jnp.logical_not(has_down))
    def _():
        clear(height + 1)

    def spread_halo(n):
        for side in range(2):
            @pl.when(has(side))
            def _():
                halo_z(n, side).wait_recv()
                halo_own(n, side).start()
                for t, k in peers:
                    halo_c(n, side, t, k, col).start()

    spread_halo(0)

    own_copies[0].wait()
    own_copies[1].wait()
    body_copy(1, 0, 1, mate).wait_recv()

    def turn(b, _):
        block = gg[b, pl.ds(1, height), :, lanes(chip, pair)].astype(F32).reshape(height * width, pair)
        at = lax.rem(lax.broadcasted_iota(jnp.int32, block.shape, 0), jnp.int32(width))
        rows = height * width
        left = jnp.where(at == width - 1, 0.0, pltpu.roll(block, rows - 1, 0))
        right = jnp.where(at == 0, 0.0, pltpu.roll(block, 1, 0))
        where = pl.ds(pl.multiple_of(b * rows, rows), rows)
        for c, part in enumerate((left, block, right)):
            turned[c * pair:(c + 1) * pair, where] = part.T.astype(BF16)
        return 0

    lax.fori_loop(0, half, turn, 0)

    def wait_halos(n, t):
        for side in range(2):
            @pl.when(has(side))
            def _():
                for k in range(2):
                    if (t, k) == (0, 0):
                        halo_own(n, side).wait()
                    else:
                        halo_c(n, side, t, k, peer(t, k)).wait_recv()

    def mate_part(t):
        theirs = pl.ds(pl.multiple_of((1 - core) * ch, ch), ch)
        return remote(kgp.at[t, :, theirs], kgr.at[t], kp_send.at[t], kp_recv.at[t], row, mate)

    mine = pl.ds(pl.multiple_of(core * ch, ch), ch)

    def z_part(t, to, slot):
        return remote(kgp.at[t, :, mine], kgz.at[slot], kz_send.at[t], kz_recv.at[slot], to, col)

    def add_in(t, other):
        def add(i, _):
            kgp[t, i, mine] = kgp[t, i, mine] + other[i]
            return 0

        lax.fori_loop(0, taps, add, 0)

    def pair_sum(t):
        mate_part(t).wait_recv()
        add_in(t, kgr.at[t])

    def relay(t):
        z_part(t, beside, t).wait_recv()
        add_in(t, kgz.at[t])
        z_part(t, blocks[t], 3).start()

    own_copies[2].wait()

    @pl.when(inner)
    def _():
        weights_z(beside, 2, across).wait_recv()
        weights_z(beside, 2, across).start()
        weights_z(across, 3, beside).wait_recv()
        weights_z(across, 3, beside).start()

    def neighbours(n):
        for t in range(3):
            for k in range(2):
                if t:
                    body_copy(n, t, k, peer(t, k)).wait_recv()
            wait_halos(n, t)
            if t:
                pass_on(n, t - 1).start()

    neighbours(0)
    for t, k in peers:
        if t:
            body_copy(1, t, k, col).start()
    spread_halo(1)

    @pl.when(inner)
    def _():
        weights_z(far, 4, beside).wait_recv()
        weights_z(far, 4, beside).start()

    @pl.when(jnp.logical_not(inner))
    def _():
        for source in (beside, across, far):
            weights_z(source, 0, beside).wait_recv()

    def weights_mate(k):
        mine = lanes(core if k == 0 else 1 - core, ch)
        return remote(wf.at[:, mine], wf.at[:, mine], wp_send, wp_recv, row, mate)

    def weights_c(t, source):
        return remote(
            wf.at[:, lanes(core, ch), lanes(chips[t], pair)], wb.at[:, lanes(source, ch)],
            wc_send.at[t], wc_recv.at[t], row, peer(t, 0),
        )

    weights_mate(0).start()
    wb_own = pltpu.make_async_copy(wf.at[:, lanes(core, ch), lanes(chip, pair)], wb.at[:, lanes(col, ch)], own_sem.at[3])
    wb_own.start()
    for t in range(1, 4):
        weights_c(t, col).start()
    body_copy(0, 0, 1, mate).wait_recv()
    passed(0, 0).wait_recv()
    passed(0, 1).wait_recv()

    for t in range(4):
        def tap_row(a, _):
            window = xg[:, pl.ds(a, height), :, lanes(blocks[t], pair)].reshape(half * height * width, pair)
            part = jnp.dot(turned[...], window, preferred_element_type=F32)
            for c in range(3):
                kgp[t, a * 3 + c] = part[c * pair:(c + 1) * pair]
            return 0

        lax.fori_loop(0, 3, tap_row, 0)
        mate_part(t).start()
        if t:
            pair_sum(t - 1)
        if t == 1:
            @pl.when(jnp.logical_not(inner))
            def _():
                z_part(0, beside, 0).start()
        if t == 3:
            @pl.when(inner)
            def _():
                z_part(2, beside, 2).start()
    pair_sum(3)

    def keep(i, _):
        kg_ref[i] = kgp[3, i, mine]
        return 0

    lax.fori_loop(0, taps, keep, 0)
    @pl.when(inner)
    def _():
        relay(0)

    @pl.when(jnp.logical_not(inner))
    def _():
        z_part(0, beside, 0).wait_send()
        z_part(1, beside, 1).start()

    neighbours(1)

    def weights_pass(t, k):
        rows = lanes(peer(t, k), ch)
        return remote(wb.at[:, rows], wb.at[:, rows], wq_send.at[t], wq_recv.at[t], row, mate)

    def result_mate(n, result, batch_half, b):
        return remote(
            stage.at[n, b], result.at[batch_half * half + b], op_send.at[n, b], op_recv.at[n, b], row, mate
        )

    def convolve(grid_ref, weights, dims, flip, result, n, parts, start, finish):
        def image(b, _):
            sums = []
            for c in range(3):
                total = None
                for a in range(3):
                    for t in parts:
                        at = slice(None) if t is None else lanes(chips[t], pair)
                        block = grid_ref[b, pl.ds(2 - a if flip else a, height), :, at]
                        block = block.reshape(height * width, block.shape[2])
                        tap = weights[a * 3 + c] if t is None else weights[a * 3 + c, at]
                        part = lax.dot_general(block, tap, (dims, ((), ())), preferred_element_type=F32)
                        total = part if total is None else total + part
                sums.append(total)
            if flip:
                sums = sums[::-1]
            value = shift_sum(*sums, width)
            if not start:
                value = value + held[b]
            if not finish:
                held[b] = value
                return 0
            value = value.astype(BF16).reshape(height, width, pair)

            @pl.when(core == 0)
            def _():
                result[b] = value[:, :, :ch]
                stage[n, b] = value[:, :, ch:]

            @pl.when(core == 1)
            def _():
                result[half + b] = value[:, :, ch:]
                stage[n, b] = value[:, :, :ch]

            result_mate(n, result, core, b).start()
            return 0

        lax.fori_loop(0, half, image, 0)

    weights_mate(1).wait_recv()
    convolve(xg, wf, ((1,), (1,)), False, out_ref, 0, (None,), True, True)

    wb_own.wait()
    weights_pass(0, 0).start()
    for t in range(1, 3):
        weights_c(t, peer(t, 0)).wait_recv()
        weights_pass(t, 0).start()
    @pl.when(inner)
    def _():
        relay(1)

    @pl.when(jnp.logical_not(inner))
    def _():
        z_part(1, beside, 1).wait_send()
        z_part(2, beside, 2).start()

    for t in range(3):
        weights_pass(t, 1).wait_recv()
    convolve(gg, wb, ((1,), (0,)), True, ig_ref, 1, (0, 1, 2), True, False)
    weights_c(3, peer(3, 0)).wait_recv()
    weights_pass(3, 0).start()

    passed(1, 0).wait_recv()
    passed(1, 1).wait_recv()
    weights_pass(3, 1).wait_recv()
    convolve(gg, wb, ((1,), (0,)), True, ig_ref, 1, (3,), False, True)

    for slot in (2, 3):
        z_part(0, beside, slot).wait_recv()

        def add(i, _):
            kg_ref[i] = kg_ref[i] + kgz[slot, i]
            return 0

        lax.fori_loop(0, taps, add, 0)

    for n in range(2):
        for t, k in peers:
            body_copy(n, t, k, col).wait_send()
        for side in range(2):
            @pl.when(has(1 - side))
            def _():
                halo_z(n, side).wait_send()

            @pl.when(has(side))
            def _():
                for t, k in peers:
                    halo_c(n, side, t, k, col).wait_send()
        for side in range(2):
            pass_on(n, side).wait_send()
    weights_own(0, beside).wait_send()

    @pl.when(inner)
    def _():
        for index in range(1, 5):
            weights_own(index, beside).wait_send()

    weights_mate(0).wait_send()
    for t in range(1, 4):
        weights_c(t, col).wait_send()
    for t in range(4):
        weights_pass(t, 0).wait_send()
        mate_part(t).wait_send()

    z_part(2, beside, 2).wait_send()

    @pl.when(inner)
    def _():
        for t in range(2):
            z_part(t, beside, t).wait_send()

    def settle(b, _):
        for n, result in enumerate((out_ref, ig_ref)):
            result_mate(n, result, core, b).wait_send()
            result_mate(n, result, 1 - core, b).wait_recv()
        return 0

    lax.fori_loop(0, half, settle, 0)


def fused(images, upstream, weights):
    n_row, n_col = lax.axis_size("row"), lax.axis_size("col")
    batch, height, width, ch = images.shape
    taps, pair, half = weights.shape[0], 2 * ch, batch // 2
    every = ch * n_col
    dma = pltpu.SemaphoreType.DMA
    vmem = pl.BlockSpec(memory_space=pltpu.VMEM)
    grid = (half, height + 2, width, every)
    flops = 3 * 2 * half * height * width * every * pair * taps
    return pl.pallas_call(
        functools.partial(kernel, n_row),
        out_shape=(
            jax.ShapeDtypeStruct(images.shape, BF16),
            jax.ShapeDtypeStruct(images.shape, BF16),
            jax.ShapeDtypeStruct(weights.shape, F32),
        ),
        in_specs=[vmem] * 3,
        out_specs=(vmem,) * 3,
        scratch_shapes=[
            pltpu.VMEM(grid, BF16),
            pltpu.VMEM(grid, BF16),
            pltpu.VMEM((taps, pair, every), BF16),
            pltpu.VMEM((taps, every, pair), BF16),
            pltpu.VMEM((2, 2, batch, 1, width, ch), BF16),
            pltpu.VMEM((3 * pair, half * height * width), BF16),
            pltpu.VMEM((4, taps, pair, pair), F32),
            pltpu.VMEM((4, taps, ch, pair), F32),
            pltpu.VMEM((n_row, taps, ch, pair), F32),
            pltpu.VMEM((2, half, height, width, ch), BF16),
            pltpu.VMEM((half, height * width, pair), F32),
            dma((4,)),
            dma((2, 4, 2)), dma((2, 4, 2)),
            dma((2, 2)), dma((2, 2)),
            dma((2, 2)), dma((2, 2)),
            dma((2, 2, 4, 2)), dma((2, 2, 4, 2)),
            dma((5,)), dma((n_row,)),
            dma, dma,
            dma((4,)), dma((4,)),
            dma((4,)), dma((4,)),
            dma((4,)), dma((4,)),
            dma((4,)), dma((n_row,)),
            dma((2, half)), dma((2, half)),
        ],
        compiler_params=pltpu.CompilerParams(
            collective_id=0, has_side_effects=True, vmem_limit_bytes=60 * 1024 * 1024
        ),
        cost_estimate=pl.CostEstimate(flops=flops, bytes_accessed=8 * 1024 * 1024, transcendentals=0),
    )(images, upstream, weights)


def fits(n_row, n_col, images, kernel_block):
    ch = images.shape[2] // W
    return (
        n_row == 4 and n_col == 8 and ch == 128 and images.shape[0] % 4 == 0
        and kernel_block.shape[2] == ch and kernel_block.shape[3] == 2 * ch and images.size <= 8 * 8 * 8192
    )


def to_last(flat):
    return to_maps(flat).transpose(0, 1, 3, 2)


def from_last(maps):
    return to_flat(maps.transpose(0, 1, 3, 2))


def padded_2(block, sides, width):
    for axis, dim in sides:
        count = lax.axis_size(axis)
        forward = [(i, i + 1) for i in range(count - 1)]
        backward = [(target, source) for source, target in forward]
        low = lax.ppermute(
            lax.slice_in_dim(block, block.shape[dim] - width, None, axis=dim), axis, forward
        )
        high = lax.ppermute(lax.slice_in_dim(block, 0, width, axis=dim), axis, backward)
        block = jnp.concatenate([low, block, high], axis=dim)
    return block


def convolve_valid(inputs, weights, weight_spec):
    return lax.conv_general_dilated(
        inputs,
        weights,
        (1, 1),
        ((0, 0), (1, 1)),
        dimension_numbers=("NHCW", weight_spec, "NHCW"),
        preferred_element_type=jnp.float32,
    )


def to_maps(flat):
    return flat.reshape(flat.shape[0], flat.shape[1], flat.shape[2] // W, W)


def to_flat(maps):
    return maps.reshape(maps.shape[0], maps.shape[1], maps.shape[2] * maps.shape[3])


def gathered(images, kernel, upstream):
    weights_all = lax.all_gather(kernel, "row", axis=3, tiled=True)
    images_rim = padded_2(images, (("row", 1),), 1)
    grads_rim = padded_2(upstream, (("row", 1),), 1)
    grads_maps = to_maps(grads_rim)
    batch = images.shape[0]
    height = images.shape[1]
    width = W
    out_local = kernel.shape[2]
    grads_mid = grads_maps[:, 1:-1]
    output_init = jnp.zeros((batch, height, out_local, width), jnp.float32)
    output_sum = output_init
    panel_in = to_maps(lax.all_gather(images_rim, "col", axis=2, tiled=True))
    count_here = panel_in.shape[2]
    output_sum = output_sum + convolve_valid(panel_in, weights_all, "HWOI")
    padded = jnp.pad(panel_in, ((0, 0), (0, 0), (0, 0), (1, 1)))
    blocks = []
    for tap_row in range(3):
        for tap_col in range(3):
            window = padded[:, tap_row : tap_row + height, :, tap_col : tap_col + width]
            blocks.append(
                jnp.einsum("bhiw,bhow->oi", window, grads_mid, preferred_element_type=jnp.float32)
            )
    stacked = jnp.stack(blocks).reshape(3, 3, out_local, count_here)
    output_sum, weight_part = (output_sum, stacked)
    kernel_grad = lax.psum_scatter(weight_part, "row", scatter_dimension=3, tiled=True)
    flipped = jnp.flip(weights_all, (0, 1))
    partial_grad = to_flat(convolve_valid(grads_maps, flipped, "HWIO"))
    input_grad = lax.psum_scatter(partial_grad, "col", scatter_dimension=2, tiled=True)
    return (to_flat(output_sum).astype(jnp.bfloat16), input_grad.astype(jnp.bfloat16), kernel_grad)


def shards(images, kernel_block, upstream):
    if not fits(lax.axis_size("row"), lax.axis_size("col"), images, kernel_block):
        return gathered(images, kernel_block, upstream)
    taps = kernel_block.reshape((9,) + kernel_block.shape[2:])
    out, grad, kernel_grad = fused(to_last(images), to_last(upstream), taps)
    return from_last(out), from_last(grad), kernel_grad.reshape(kernel_block.shape)


def solution(mesh):
    return jax.shard_map(
        shards,
        mesh=mesh,
        in_specs=(P(None, "row", "col"), P(None, None, "col", "row"), P(None, "row", "col")),
        out_specs=(P(None, "row", "col"), P(None, "row", "col"), P(None, None, "col", "row")),
        check_vma=False,
    )
```
